256 devices in a mesh: dp: 16 (over x_hi, y, core), seq: 16 (over z, x_lo).
Axes of the slice: x: 4 (x_hi: 2, x_lo: 2; x = x_hi * 2 + x_lo), y: 4, z: 8, core: 2. Of those that a mesh axis runs over, the one named last changes fastest.
Arguments:
- clip_tokens: bfloat16 [16, 16, 768, 1152], P('dp', 'seq'), may hold values from -6 to 6
- time_mod: float32 [16, 3, 1152], P('dp'), may hold values from -2 to 4
- mod_table: float32 [3, 1152], replicated, may hold values from -3 to 3
- w_qkv: bfloat16 [1152, 1728], replicated, may hold values from -0.1875 to 0.1875
- w_out: bfloat16 [576, 1152], replicated, may hold values from -0.25 to 0.25
- out_grad: bfloat16 [16, 16, 768, 1152], P('dp', 'seq'), may hold values from -6 to 6
Outputs:
- out_tokens: bfloat16 [16, 16, 768, 1152], P('dp', 'seq')
- grad_tokens: bfloat16 [16, 16, 768, 1152], P('dp', 'seq')
- grad_qkv_weight: float32 [1152, 1728], P('seq')
- grad_out_weight: float32 [576, 1152], P('seq')
- grad_table: float32 [3, 1152], replicated
The draws below stay inside these ranges and needn't reach their ends.
All inputs are finite; a program needn't handle non-finite values.
Results may differ from the reference program's by a relative error of at most 0.0095.
The reference program's roundings to bfloat16 on the way count: a program that leaves them out, or rounds other values in their place, can miss the bound.
Values may be sent and summed in bfloat16 or wider, within the bound.
No kernel may reach another device: no remote copies, remote signals or barrier semaphores. Data moves between devices by JAX's collectives and lax.ppermute only.
A program may use at most 128 MiB of HBM per device.

```python
import math
import jax
import jax.numpy as jnp
from jax import lax

D = 1152
HEAD_DIM = 72
HEADS = 8
POS = 768
INNER = 576
FRAMES = 16
CLIPS = 16


def draw_time_mod(key, part):
    key = jax.random.fold_in(key, 7)
    key_rows = jax.random.fold_in(key, 0)
    return jnp.clip(0.5 * jax.random.normal(key_rows, (CLIPS, 3, D), jnp.float32), -2.0, 2.0)


def block_scale(rng, dims, cuts, least, largest):
    gain = 1.0
    for axis_at, blocks in cuts:
        draws = jax.random.uniform(jax.random.fold_in(jax.random.fold_in(rng, 6), axis_at), (blocks,), jnp.float32, least / len(cuts), largest / len(cuts))
        gain = gain * jnp.repeat(jnp.exp(draws), dims[axis_at] // blocks).reshape((-1,) + (1,) * (len(dims) - 1 - axis_at))
    return gain


def centred(key, extent, scale, bound, cuts=(), held_as=jnp.bfloat16):
    result = scale * jax.random.normal(key, extent, jnp.float32)
    if cuts:
        result = result * block_scale(key, extent, cuts, -0.22, 0.18)
    return jnp.clip(result, -bound, bound).astype(held_as)


def setup_inputs(seed: int = 0) -> dict:
    key_list = jax.random.split(jax.random.key(seed), 7)
    return {
        "clip_tokens": centred(key_list[0], (CLIPS, FRAMES, POS, D), 1.0, 6.0, ((0, 16), (1, 16))),
        "time_mod": draw_time_mod(jax.random.fold_in(key_list[6], 71), 0),
        "mod_table": centred(key_list[2], (3, D), 0.5, 3.0, (), jnp.float32),
        "w_qkv": centred(key_list[3], (D, 3 * INNER), D ** -0.5, 0.1875),
        "w_out": centred(key_list[4], (INNER, D), INNER ** -0.5, 0.25),
        "out_grad": centred(key_list[5], (CLIPS, FRAMES, POS, D), 1.0, 6.0, ((0, 16), (1, 16))),
    }


EPSILON = 1e-06

def split_heads(packed):
    frames, positions = (packed.shape[0], packed.shape[1])
    return packed.reshape(frames, positions, 3, HEADS, HEAD_DIM).astype(jnp.float32)

def attend(packed):
    pieces = split_heads(packed)
    queries, key_rows, values = (pieces[:, :, 0], pieces[:, :, 1], pieces[:, :, 2])
    scores = jnp.einsum('fmne,gmne->fmng', queries, key_rows) / math.sqrt(HEAD_DIM)
    row_max = lax.optimization_barrier(jnp.max(scores, axis=3, keepdims=True))
    exp_scores = jnp.exp(scores - row_max)
    weights = exp_scores / lax.optimization_barrier(jnp.sum(exp_scores, axis=3, keepdims=True))
    probs = lax.optimization_barrier(weights.astype(jnp.bfloat16)).astype(jnp.float32)
    mixed = jnp.einsum('fmng,gmne->fmne', probs, values)
    return (mixed.astype(jnp.bfloat16).reshape(packed.shape[0], packed.shape[1], INNER), weights)

def attend_grad(packed, weights, grad_mixed):
    frames, positions = (packed.shape[0], packed.shape[1])
    pieces = split_heads(packed)
    queries, key_rows, values = (pieces[:, :, 0], pieces[:, :, 1], pieces[:, :, 2])
    grad_heads = grad_mixed.reshape(frames, positions, HEADS, HEAD_DIM).astype(jnp.float32)
    probs = lax.optimization_barrier(weights.astype(jnp.bfloat16)).astype(jnp.float32)
    grad_weights = jnp.einsum('fmne,gmne->fmng', grad_heads, values)
    grad_values = jnp.einsum('fmng,fmne->gmne', probs, grad_heads).astype(jnp.bfloat16)
    row_total = lax.optimization_barrier(jnp.sum(weights * grad_weights, axis=3, keepdims=True))
    grad_scores = (weights * (grad_weights - row_total) / math.sqrt(HEAD_DIM)).astype(jnp.bfloat16)
    grad_scores = lax.optimization_barrier(grad_scores).astype(jnp.float32)
    grad_queries = jnp.einsum('fmng,gmne->fmne', grad_scores, key_rows).astype(jnp.bfloat16)
    grad_keys = jnp.einsum('fmng,fmne->gmne', grad_scores, queries).astype(jnp.bfloat16)
    stacked = jnp.stack([grad_queries, grad_keys, grad_values], axis=2)
    return stacked.reshape(frames, positions, 3 * INNER)

def clip_pass(clip_rows, time_rows, grad_rows, mod_table, w_qkv, w_out):
    modulation = mod_table + time_rows
    shift_row, scale_row, gate_row = (modulation[0], modulation[1], modulation[2])
    tokens_wide = clip_rows.astype(jnp.float32).reshape(FRAMES * POS, D)
    row_mean = lax.optimization_barrier(jnp.mean(tokens_wide, axis=1, keepdims=True))
    centered = tokens_wide - row_mean
    row_var = lax.optimization_barrier(jnp.mean(centered * centered, axis=1, keepdims=True))
    inv_std = lax.rsqrt(row_var + EPSILON)
    normed = centered * inv_std
    modulated = (normed * (1.0 + scale_row) + shift_row).astype(jnp.bfloat16)
    packed = jnp.dot(modulated, w_qkv, preferred_element_type=jnp.float32).astype(jnp.bfloat16)
    packed = packed.reshape(FRAMES, POS, 3 * INNER)
    mixed, weights = attend(packed)
    mixed_flat = mixed.reshape(FRAMES * POS, INNER)
    branch = jnp.dot(mixed_flat, w_out, preferred_element_type=jnp.float32)
    out_tokens = (tokens_wide + gate_row * branch).astype(jnp.bfloat16)
    grad_out = grad_rows.astype(jnp.float32).reshape(FRAMES * POS, D)
    grad_gate = lax.optimization_barrier(jnp.sum(grad_out * branch, axis=0))
    grad_branch = (grad_out * gate_row).astype(jnp.bfloat16)
    out_term = jnp.dot(mixed_flat.T, grad_branch, preferred_element_type=jnp.float32)
    grad_mixed = jnp.dot(grad_branch, w_out.T, preferred_element_type=jnp.float32).astype(jnp.bfloat16)
    grad_packed = attend_grad(packed, weights, grad_mixed.reshape(FRAMES, POS, INNER))
    grad_flat = grad_packed.reshape(FRAMES * POS, 3 * INNER)
    qkv_term = jnp.dot(modulated.T, grad_flat, preferred_element_type=jnp.float32)
    grad_mod = jnp.dot(grad_flat, w_qkv.T, preferred_element_type=jnp.float32)
    grad_shift = lax.optimization_barrier(jnp.sum(grad_mod, axis=0))
    grad_scale = lax.optimization_barrier(jnp.sum(grad_mod * normed, axis=0))
    grad_normed = grad_mod * (1.0 + scale_row)
    grad_tokens = grad_out + inv_std * (grad_normed - lax.optimization_barrier(jnp.mean(grad_normed, axis=1, keepdims=True)) - normed * lax.optimization_barrier(jnp.mean(grad_normed * normed, axis=1, keepdims=True)))
    table_term = jnp.stack([grad_shift, grad_scale, grad_gate])
    return (out_tokens.reshape(FRAMES, POS, D), grad_tokens.astype(jnp.bfloat16).reshape(FRAMES, POS, D), qkv_term, out_term, table_term)

def reference(clip_tokens, time_mod, mod_table, w_qkv, w_out, out_grad):

    def one_clip(inputs):
        return clip_pass(inputs[0], inputs[1], inputs[2], mod_table, w_qkv, w_out)
    out_tokens, grad_tokens, qkv_terms, out_terms, table_terms = lax.map(one_clip, (clip_tokens, time_mod, out_grad))
    factor = 1.0 / math.sqrt(CLIPS * FRAMES * POS)
    grad_qkv_weight = lax.optimization_barrier(jnp.sum(qkv_terms, axis=0)) * factor
    grad_out_weight = lax.optimization_barrier(jnp.sum(out_terms, axis=0)) * factor
    grad_table = lax.optimization_barrier(jnp.sum(table_terms, axis=0)) * factor
    return (out_tokens, grad_tokens, grad_qkv_weight, grad_out_weight, grad_table)
```

```python
import functools
import math

import jax
import jax.numpy as jnp
from jax import lax
from jax.experimental import pallas as pl
from jax.experimental.pallas import tpu as pltpu
from jax.sharding import PartitionSpec as P

D = 1152
HEAD_DIM = 72
HEADS = 8
POS = 768
INNER = 576
SEQ = 16
DP = 16
HERE = POS // SEQ
TILE = 16
ROWS = SEQ * TILE
STEPS = HERE // TILE
EPSILON = 1e-06
SCALE = 1.0 / math.sqrt(HEAD_DIM)
BF = jnp.bfloat16
F32 = jnp.float32
PARAMS = pltpu.CompilerParams(
    dimension_semantics=("arbitrary",), vmem_limit_bytes=56 * 1024 * 1024
)
NT = (((1,), (1,)), ((), ()))
TN = (((0,), (0,)), ((), ()))


def dot(a, b, dims=(((1,), (0,)), ((), ()))):
    return lax.dot_general(a, b, dims, preferred_element_type=F32)


def normalize(x):
    centered = x - jnp.mean(x, axis=1, keepdims=True)
    inv_std = lax.rsqrt(jnp.mean(centered * centered, axis=1, keepdims=True) + EPSILON)
    return centered * inv_std, inv_std


def position_mask():
    rows = lax.broadcasted_iota(jnp.int32, (ROWS, ROWS), 0) % TILE
    cols = lax.broadcasted_iota(jnp.int32, (ROWS, ROWS), 1) % TILE
    return jnp.where(rows == cols, 0.0, -1e30).astype(F32)


def softmax(queries, key_rows, mask):
    scores = dot(queries, key_rows, NT) * SCALE + mask
    exp_scores = jnp.exp(scores - jnp.max(scores, axis=1, keepdims=True))
    return exp_scores * (1.0 / jnp.sum(exp_scores, axis=1, keepdims=True))


def head(array, part, n):
    start = part * INNER + n * HEAD_DIM
    return array[:, start : start + HEAD_DIM]


def forward_kernel(x_ref, mod_ref, w_ref, packed_ref, mixed_ref):
    normed, _ = normalize(x_ref[...].reshape(ROWS, D).astype(F32))
    modulated = (normed * (1.0 + mod_ref[1:2, :]) + mod_ref[0:1, :]).astype(BF)
    packed = dot(modulated, w_ref[...]).astype(BF)
    packed_ref[...] = packed.reshape(SEQ, TILE, 3 * INNER)
    mask = position_mask()
    pieces = []
    for n in range(HEADS):
        weights = softmax(head(packed, 0, n), head(packed, 1, n), mask)
        pieces.append(dot(weights.astype(BF), head(packed, 2, n)).astype(BF))
    mixed_ref[...] = jnp.concatenate(pieces, axis=1).reshape(SEQ, TILE, INNER)


def forward(x, modulation, w_qkv):
    return pl.pallas_call(
        forward_kernel,
        grid=(STEPS,),
        in_specs=[
            pl.BlockSpec((SEQ, TILE, D), lambda j: (0, j, 0)),
            pl.BlockSpec((3, D), lambda j: (0, 0)),
            pl.BlockSpec((D, 3 * INNER), lambda j: (0, 0)),
        ],
        out_specs=[
            pl.BlockSpec((SEQ, TILE, 3 * INNER), lambda j: (0, j, 0)),
            pl.BlockSpec((SEQ, TILE, INNER), lambda j: (0, j, 0)),
        ],
        out_shape=[
            jax.ShapeDtypeStruct((SEQ, HERE, 3 * INNER), BF),
            jax.ShapeDtypeStruct((SEQ, HERE, INNER), BF),
        ],
        compiler_params=PARAMS,
        cost_estimate=pl.CostEstimate(
            flops=2 * POS * D * 3 * INNER * 3, bytes_accessed=12_000_000, transcendentals=1_600_000
        ),
        name="forward",
    )(x, modulation, w_qkv)


def backward_kernel(
    core_ref, x_ref, packed_ref, gm_ref, mod_ref, w_ref,
    delta_ref, keep_ref, send_ref, table_ref,
    modulated_all, gp_all, total,
):
    step = pl.program_id(0)
    normed, inv_std = normalize(x_ref[...].reshape(ROWS, D).astype(F32))
    scale_row = 1.0 + mod_ref[1:2, :]
    modulated_all[pl.ds(step * ROWS, ROWS), :] = (normed * scale_row + mod_ref[0:1, :]).astype(BF)
    packed = packed_ref[...].reshape(ROWS, 3 * INNER)
    grad_mixed = gm_ref[...].reshape(ROWS, INNER)
    mask = position_mask()
    pieces = [[], [], []]
    for n in range(HEADS):
        queries, key_rows, values = (head(packed, part, n) for part in range(3))
        weights = softmax(queries, key_rows, mask)
        grad_head = head(grad_mixed, 0, n)
        grad_weights = dot(grad_head, values, NT)
        row_total = jnp.sum(weights * grad_weights, axis=1, keepdims=True)
        grad_scores = (weights * (grad_weights - row_total) * SCALE).astype(BF)
        pieces[0].append(dot(grad_scores, key_rows).astype(BF))
        pieces[1].append(dot(grad_scores, queries, TN).astype(BF))
        pieces[2].append(dot(weights.astype(BF), grad_head, TN).astype(BF))
    grad_packed = jnp.concatenate(pieces[0] + pieces[1] + pieces[2], axis=1)
    gp_all[pl.ds(step * ROWS, ROWS), :] = grad_packed
    grad_mod = dot(grad_packed, w_ref[...], NT)
    shift_sum = jnp.sum(grad_mod, axis=0, keepdims=True)
    scale_sum = jnp.sum(grad_mod * normed, axis=0, keepdims=True)
    grad_normed = grad_mod * scale_row
    delta = inv_std * (
        grad_normed
        - jnp.mean(grad_normed, axis=1, keepdims=True)
        - normed * jnp.mean(grad_normed * normed, axis=1, keepdims=True)
    )
    delta_ref[...] = delta.astype(BF).reshape(SEQ, TILE, D)

    @pl.when(step == 0)
    def _():
        table_ref[...] = jnp.zeros_like(table_ref)

    table_ref[0:1, :] += shift_sum
    table_ref[1:2, :] += scale_sum

    @pl.when(step == STEPS - 1)
    def _():
        for r in range(3):
            part = slice(r * 384, r * 384 + 384)
            total[part, :] = dot(modulated_all[:, part], gp_all[...], TN)
        core = core_ref[0]
        rows = D // DP
        for k in range(DP // 2):
            mine = pl.multiple_of((2 * k + core) * rows, 8)
            other = pl.multiple_of((2 * k + 1 - core) * rows, 8)
            keep_ref[k] = total[pl.ds(mine, rows), :].astype(BF)
            send_ref[k] = total[pl.ds(other, rows), :].astype(BF)


def backward(core, x, packed, grad_mixed, modulation, w_qkv):
    rows = D // DP
    half = jax.ShapeDtypeStruct((DP // 2, rows, 3 * INNER), BF)
    return pl.pallas_call(
        backward_kernel,
        grid=(STEPS,),
        in_specs=[
            pl.BlockSpec(memory_space=pltpu.SMEM),
            pl.BlockSpec((SEQ, TILE, D), lambda j: (0, j, 0)),
            pl.BlockSpec((SEQ, TILE, 3 * INNER), lambda j: (0, j, 0)),
            pl.BlockSpec((SEQ, TILE, INNER), lambda j: (0, j, 0)),
            pl.BlockSpec((3, D), lambda j: (0, 0)),
            pl.BlockSpec((D, 3 * INNER), lambda j: (0, 0)),
        ],
        out_specs=[
            pl.BlockSpec((SEQ, TILE, D), lambda j: (0, j, 0)),
            pl.BlockSpec(half.shape, lambda j: (0, 0, 0)),
            pl.BlockSpec(half.shape, lambda j: (0, 0, 0)),
            pl.BlockSpec((8, D), lambda j: (0, 0)),
        ],
        out_shape=[
            jax.ShapeDtypeStruct((SEQ, HERE, D), BF),
            half,
            half,
            jax.ShapeDtypeStruct((8, D), F32),
        ],
        scratch_shapes=[
            pltpu.VMEM((POS, D), BF),
            pltpu.VMEM((POS, 3 * INNER), BF),
            pltpu.VMEM((D, 3 * INNER), F32),
        ],
        compiler_params=PARAMS,
        cost_estimate=pl.CostEstimate(
            flops=2 * POS * D * 3 * INNER * 5, bytes_accessed=20_000_000, transcendentals=1_600_000
        ),
        name="backward",
    )(core, x, packed, grad_mixed, modulation, w_qkv)


def output_kernel(
    core_ref, mixed_ref, x_ref, grad_ref, mod_ref, w_ref, out_ref, keep_ref, send_ref, gate_ref, total
):
    step = pl.program_id(0)
    gate_row = mod_ref[2:3, :]
    mixed = mixed_ref[...]
    branch = dot(mixed, w_ref[...])
    out_ref[...] = (x_ref[...].astype(F32) + gate_row * branch).astype(BF)
    grad_out = grad_ref[...].astype(F32)
    gate_sum = jnp.sum(grad_out * branch, axis=0, keepdims=True)
    term = dot(mixed, (grad_out * gate_row).astype(BF), TN)

    @pl.when(step == 0)
    def _():
        total[...] = jnp.zeros_like(total)
        gate_ref[...] = jnp.zeros_like(gate_ref)

    total[...] += term
    gate_ref[0:1, :] += gate_sum

    @pl.when(step == POS // ROWS - 1)
    def _():
        rows = INNER // DP
        core = core_ref[0]
        for k in range(DP // 2):
            both = total[2 * k * rows : 2 * (k + 1) * rows, :]
            first, second = both[:rows].astype(BF), both[rows:].astype(BF)
            keep_ref[k] = jnp.where(core == 0, first, second)
            send_ref[k] = jnp.where(core == 0, second, first)


def output(core, mixed, x, out_grad, modulation, w_out):
    half = jax.ShapeDtypeStruct((DP // 2, INNER // DP, D), BF)
    return pl.pallas_call(
        output_kernel,
        grid=(POS // ROWS,),
        in_specs=[
            pl.BlockSpec(memory_space=pltpu.SMEM),
            pl.BlockSpec((ROWS, INNER), lambda j: (j, 0)),
            pl.BlockSpec((ROWS, D), lambda j: (j, 0)),
            pl.BlockSpec((ROWS, D), lambda j: (j, 0)),
            pl.BlockSpec((3, D), lambda j: (0, 0)),
            pl.BlockSpec((INNER, D), lambda j: (0, 0)),
        ],
        out_specs=[
            pl.BlockSpec((ROWS, D), lambda j: (j, 0)),
            pl.BlockSpec(half.shape, lambda j: (0, 0, 0)),
            pl.BlockSpec(half.shape, lambda j: (0, 0, 0)),
            pl.BlockSpec((8, D), lambda j: (0, 0)),
        ],
        out_shape=[
            jax.ShapeDtypeStruct((POS, D), BF),
            half,
            half,
            jax.ShapeDtypeStruct((8, D), F32),
        ],
        scratch_shapes=[pltpu.VMEM((INNER, D), F32)],
        compiler_params=PARAMS,
        cost_estimate=pl.CostEstimate(
            flops=4 * POS * D * INNER, bytes_accessed=9_000_000, transcendentals=0
        ),
        name="output",
    )(core, mixed, x, out_grad, modulation, w_out)


def exchange(blocks, axis, groups=None):
    return lax.all_to_all(blocks, axis, 0, 0, axis_index_groups=groups, tiled=True)


def wide_sum(blocks):
    return jnp.sum(blocks.astype(F32), axis=0)


def body(clip_tokens, time_mod, mod_table, w_qkv, w_out, out_grad):
    tokens, grad_rows = clip_tokens[0, 0], out_grad[0, 0]
    modulation = mod_table + time_mod[0]
    core = lax.rem(lax.axis_index("dp"), 2).astype(jnp.int32).reshape(1)
    x_pos = exchange(tokens.reshape(SEQ, HERE, D), "seq")
    grad_branch = (grad_rows.astype(F32) * modulation[2]).astype(BF)
    grad_mixed = dot(grad_branch, w_out, NT).astype(BF)
    gm_pos = exchange(grad_mixed.reshape(SEQ, HERE, INNER), "seq")
    packed, mixed_pos = forward(x_pos, modulation, w_qkv)
    mixed = exchange(mixed_pos, "seq").reshape(POS, INNER)
    delta_pos, qkv_keep, qkv_send, table2 = backward(core, x_pos, packed, gm_pos, modulation, w_qkv)
    delta = exchange(delta_pos, "seq").reshape(POS, D)
    out_tokens, out_keep, out_send, gate_sum = output(
        core, mixed, tokens, grad_rows, modulation, w_out
    )
    grad_tokens = (grad_rows.astype(F32) + delta.astype(F32)).astype(BF)

    factor = 1.0 / math.sqrt(DP * SEQ * POS)
    swap = [(i, i ^ 1) for i in range(DP)]
    chips = [[2 * k + c for k in range(DP // 2)] for c in range(2)]
    table = jnp.concatenate([table2[0:2], gate_sum[0:1]], axis=0)

    def over_dp(keep, send):
        pair = keep.astype(F32) + lax.ppermute(send, "dp", swap).astype(F32)
        return wide_sum(exchange(pair.astype(BF), "dp", chips))

    qkv_block = over_dp(qkv_keep, qkv_send)
    out_block = over_dp(out_keep, out_send)
    table = table + lax.ppermute(table, "dp", swap)
    table = wide_sum(exchange(jnp.broadcast_to(table[None], (DP // 2, 3, D)), "dp", chips))

    def pieces(block, n):
        return jnp.moveaxis(block.reshape(block.shape[0], SEQ, n), 1, 0)

    small = jnp.concatenate(
        [
            jnp.pad(pieces(qkv_block, 108), ((0, 0), (0, 0), (0, 20))),
            jnp.pad(pieces(out_block, 72), ((0, 0), (0, 4), (0, 56))),
        ],
        axis=1,
    ).astype(BF)
    small = wide_sum(exchange(small, "seq")) * factor
    table = wide_sum(exchange(jnp.broadcast_to(table[None], (SEQ, 3, D)), "seq")) * factor
    turn = [(i * SEQ + s, s * SEQ + i) for i in range(DP) for s in range(SEQ)]
    small = lax.ppermute(small, ("dp", "seq"), turn)
    small = exchange(jnp.broadcast_to(small[None], (DP,) + small.shape), "dp")
    qkv_grad = jnp.moveaxis(small[:, :72, :108], 0, 1).reshape(72, 3 * INNER)
    out_weight_grad = jnp.moveaxis(small[:, 72:108, :72], 0, 1).reshape(36, D)
    return (
        out_tokens[None, None],
        grad_tokens[None, None],
        qkv_grad,
        out_weight_grad,
        table,
    )


def solution(mesh):
    return jax.shard_map(
        body,
        mesh=mesh,
        in_specs=(
            P("dp", "seq", None, None),
            P("dp", None, None),
            P(),
            P(),
            P(),
            P("dp", "seq", None, None),
        ),
        out_specs=(
            P("dp", "seq", None, None),
            P("dp", "seq", None, None),
            P("seq", None),
            P("seq", None),
            P(),
        ),
        check_vma=False,
    )
```

```python
import functools
import math

import jax
import jax.numpy as jnp
from jax import lax
from jax.experimental import pallas as pl
from jax.experimental.pallas import tpu as pltpu
from jax.sharding import PartitionSpec as P

D = 1152
HEAD_DIM = 72
HEADS = 8
POS = 768
INNER = 576
SEQ = 16
DP = 16
CHIPS = DP // 2
HERE = POS // SEQ
TILE = 16
HALF = 8
ROWS = SEQ * TILE
UNIT = SEQ * HALF
PAIR = 2 * HEAD_DIM
QKV_ROWS = 64
OUT_ROWS = 24
BLOCK_ROWS = QKV_ROWS + OUT_ROWS
STEPS = HERE // TILE
EPSILON = 1e-06
SCALE = 1.0 / math.sqrt(HEAD_DIM)
BF = jnp.bfloat16
F32 = jnp.float32
PARAMS = pltpu.CompilerParams(
    dimension_semantics=("arbitrary",), vmem_limit_bytes=56 * 1024 * 1024
)
WHOLE = pltpu.CompilerParams(vmem_limit_bytes=40 * 1024 * 1024)
NT = (((1,), (1,)), ((), ()))
TN = (((0,), (0,)), ((), ()))


def dot(a, b, dims=(((1,), (0,)), ((), ()))):
    return lax.dot_general(a, b, dims, preferred_element_type=F32)


def normalize(x):
    centered = x - jnp.mean(x, axis=1, keepdims=True)
    inv_std = lax.rsqrt(jnp.mean(centered * centered, axis=1, keepdims=True) + EPSILON)
    return centered * inv_std, inv_std


def load_rows(block):
    wide = block.astype(F32)
    width = wide.shape[-1]
    return jnp.concatenate(
        [wide[:, :HALF].reshape(UNIT, width), wide[:, HALF:].reshape(UNIT, width)], axis=0
    )


def store_rows(rows):
    width = rows.shape[-1]
    halves = [rows[h * UNIT : h * UNIT + UNIT].reshape(SEQ, HALF, width) for h in range(2)]
    return jnp.concatenate(halves, axis=1).astype(BF)


def position_mask():
    rows = lax.broadcasted_iota(jnp.int32, (HALF, UNIT), 0)
    cols = lax.broadcasted_iota(jnp.int32, (HALF, UNIT), 1) % HALF
    return jnp.where(rows == cols, 1.0, 0.0).astype(F32)


def first_lanes(dtype):
    lanes = lax.broadcasted_iota(jnp.int32, (1, PAIR), 1)
    return jnp.where(lanes < HEAD_DIM, 1.0, 0.0).astype(dtype)


def spread(pair, first):
    return jnp.concatenate([pair * first, pair * (1 - first)], axis=0)


def gather(rows, first):
    return rows[:UNIT] * first + rows[UNIT:] * (1 - first)


def by_frame(rows):
    return rows.reshape(2, SEQ, HALF, UNIT)


def softmax(queries, keys_spread, mask):
    scores = by_frame(dot(keys_spread, queries, NT) * SCALE)
    exp_scores = jnp.exp(scores - jnp.max(scores, axis=1, keepdims=True))
    return exp_scores * (mask / jnp.sum(exp_scores, axis=1, keepdims=True))


def flat(weights):
    return weights.reshape(2 * UNIT, UNIT).astype(BF)


def pair_of(rows, part, n):
    start = part * INNER + n * PAIR
    return rows[:, start : start + PAIR]


def forward_kernel(x_ref, mod_ref, w_ref, packed_ref, mixed_ref):
    normed, _ = normalize(load_rows(x_ref[...]))
    modulated = (normed * (1.0 + mod_ref[1:2, :]) + mod_ref[0:1, :]).astype(BF)
    packed = dot(modulated, w_ref[...], NT).astype(BF)
    packed_ref[...] = packed
    mask, first = position_mask(), first_lanes(BF)
    units = []
    for u in range(2):
        rows = packed[u * UNIT : u * UNIT + UNIT]
        pieces = []
        for n in range(HEADS // 2):
            weights = softmax(pair_of(rows, 0, n), spread(pair_of(rows, 1, n), first), mask)
            pieces.append(dot(flat(weights), spread(pair_of(rows, 2, n), first), TN))
        units.append(jnp.concatenate(pieces, axis=1))
    mixed_ref[...] = store_rows(jnp.concatenate(units, axis=0))


def forward(x, modulation, w_turned):
    return pl.pallas_call(
        forward_kernel,
        grid=(STEPS,),
        in_specs=[
            pl.BlockSpec((SEQ, TILE, D), lambda j: (0, j, 0)),
            pl.BlockSpec((3, D), lambda j: (0, 0)),
            pl.BlockSpec((3 * INNER, D), lambda j: (0, 0)),
        ],
        out_specs=[
            pl.BlockSpec((ROWS, 3 * INNER), lambda j: (j, 0)),
            pl.BlockSpec((SEQ, TILE, INNER), lambda j: (0, j, 0)),
        ],
        out_shape=[
            jax.ShapeDtypeStruct((POS, 3 * INNER), BF),
            jax.ShapeDtypeStruct((SEQ, HERE, INNER), BF),
        ],
        compiler_params=PARAMS,
        cost_estimate=pl.CostEstimate(
            flops=2 * POS * D * 3 * INNER * 2, bytes_accessed=12_000_000, transcendentals=800_000
        ),
        name="forward",
    )(x, modulation, w_turned)


def grad_mixed_kernel(grad_ref, mod_ref, w_ref, out_ref):
    grad_branch = (grad_ref[...].astype(F32) * mod_ref[2:3, :]).astype(BF)
    out_ref[...] = dot(grad_branch, w_ref[...], NT).astype(BF)


def grad_mixed_rows(out_grad, modulation, w_out):
    return pl.pallas_call(
        grad_mixed_kernel,
        grid=(POS // ROWS,),
        in_specs=[
            pl.BlockSpec((ROWS, D), lambda j: (j, 0)),
            pl.BlockSpec((3, D), lambda j: (0, 0)),
            pl.BlockSpec((INNER, D), lambda j: (0, 0)),
        ],
        out_specs=pl.BlockSpec((ROWS, INNER), lambda j: (j, 0)),
        out_shape=jax.ShapeDtypeStruct((POS, INNER), BF),
        compiler_params=PARAMS,
        cost_estimate=pl.CostEstimate(
            flops=2 * POS * D * INNER, bytes_accessed=4_000_000, transcendentals=0
        ),
        name="grad_mixed",
    )(out_grad, modulation, w_out)


def backward_kernel(
    place_ref, x_ref, gm_ref, packed_ref, mod_ref, w_ref,
    delta_ref, keep_ref, send_ref, table_ref,
    modulated_all, gp_all, total,
):
    step = pl.program_id(0)
    normed, inv_std = normalize(load_rows(x_ref[...]))
    scale_row = 1.0 + mod_ref[1:2, :]
    here = pl.ds(pl.multiple_of(step * ROWS, ROWS), ROWS)
    modulated_all[here, :] = (normed * scale_row + mod_ref[0:1, :]).astype(BF)
    grad_mixed = load_rows(gm_ref[...]).astype(BF)
    packed = packed_ref[...]
    mask, first, first_wide = position_mask(), first_lanes(BF), first_lanes(F32)
    units = []
    for u in range(2):
        rows = packed[u * UNIT : u * UNIT + UNIT]
        grad_rows = grad_mixed[u * UNIT : u * UNIT + UNIT]
        pieces = [[], [], []]
        for n in range(HEADS // 2):
            queries = pair_of(rows, 0, n)
            keys_spread = spread(pair_of(rows, 1, n), first)
            values_spread = spread(pair_of(rows, 2, n), first)
            grad_pair = pair_of(grad_rows, 0, n)
            weights = softmax(queries, keys_spread, mask)
            grad_weights = by_frame(dot(values_spread, grad_pair, NT))
            row_total = jnp.sum(weights * grad_weights, axis=1, keepdims=True)
            grad_scores = flat(weights * (grad_weights - row_total) * SCALE)
            pieces[0].append(dot(grad_scores, keys_spread, TN).astype(BF))
            pieces[1].append(gather(dot(grad_scores, queries), first_wide).astype(BF))
            pieces[2].append(gather(dot(flat(weights), grad_pair), first_wide).astype(BF))
        units.append(jnp.concatenate(pieces[0] + pieces[1] + pieces[2], axis=1))
    grad_packed = jnp.concatenate(units, axis=0)
    gp_all[here, :] = grad_packed
    grad_mod = dot(grad_packed, w_ref[...])
    shift_sum = jnp.sum(grad_mod, axis=0, keepdims=True)
    scale_sum = jnp.sum(grad_mod * normed, axis=0, keepdims=True)
    grad_normed = grad_mod * scale_row
    delta = inv_std * (
        grad_normed
        - jnp.mean(grad_normed, axis=1, keepdims=True)
        - normed * jnp.mean(grad_normed * normed, axis=1, keepdims=True)
    )
    delta_ref[...] = store_rows(delta)

    @pl.when(step == 0)
    def _():
        table_ref[...] = jnp.zeros_like(table_ref)

    table_ref[0:1, :] += shift_sum
    table_ref[1:2, :] += scale_sum

    @pl.when(step == STEPS - 1)
    def _():
        for r in range(3):
            part = slice(r * 384, r * 384 + 384)
            total[part, :] = dot(modulated_all[:, part], gp_all[...], TN)
        core = place_ref[0]
        rows = D // DP
        for k in range(CHIPS):
            chip = k % 2 * 4 + k // 2
            mine = pl.multiple_of((2 * chip + core) * rows, 8)
            other = pl.multiple_of((2 * chip + 1 - core) * rows, 8)
            keep_ref[k] = total[pl.ds(mine, rows), :].astype(BF)
            send_ref[k] = total[pl.ds(other, rows), :].astype(BF)


def backward(place, x, grad_mixed, packed, modulation, w_turned):
    half = jax.ShapeDtypeStruct((CHIPS, D // DP, 3 * INNER), BF)
    return pl.pallas_call(
        backward_kernel,
        grid=(STEPS,),
        in_specs=[
            pl.BlockSpec(memory_space=pltpu.SMEM),
            pl.BlockSpec((SEQ, TILE, D), lambda j: (0, j, 0)),
            pl.BlockSpec((SEQ, TILE, INNER), lambda j: (0, j, 0)),
            pl.BlockSpec((ROWS, 3 * INNER), lambda j: (j, 0)),
            pl.BlockSpec((3, D), lambda j: (0, 0)),
            pl.BlockSpec((3 * INNER, D), lambda j: (0, 0)),
        ],
        out_specs=[
            pl.BlockSpec((SEQ, TILE, D), lambda j: (0, j, 0)),
            pl.BlockSpec(half.shape, lambda j: (0, 0, 0)),
            pl.BlockSpec(half.shape, lambda j: (0, 0, 0)),
            pl.BlockSpec((8, D), lambda j: (0, 0)),
        ],
        out_shape=[
            jax.ShapeDtypeStruct((SEQ, HERE, D), BF),
            half,
            half,
            jax.ShapeDtypeStruct((8, D), F32),
        ],
        scratch_shapes=[
            pltpu.VMEM((POS, D), BF),
            pltpu.VMEM((POS, 3 * INNER), BF),
            pltpu.VMEM((D, 3 * INNER), F32),
        ],
        compiler_params=PARAMS,
        cost_estimate=pl.CostEstimate(
            flops=2 * POS * D * 3 * INNER * 4, bytes_accessed=20_000_000, transcendentals=800_000
        ),
        name="backward",
    )(place, x, grad_mixed, packed, modulation, w_turned)


def output_kernel(
    place_ref, mixed_ref, x_ref, grad_ref, mod_ref, w_ref, table_ref,
    out_ref, keep_ref, send_ref, total, gate_total,
):
    step = pl.program_id(0)
    gate_row = mod_ref[2:3, :]
    mixed = mixed_ref[...]
    branch = dot(mixed, w_ref[...])
    out_ref[...] = (x_ref[...].astype(F32) + gate_row * branch).astype(BF)
    grad_out = grad_ref[...].astype(F32)
    gate_sum = jnp.sum(grad_out * branch, axis=0, keepdims=True)
    term = dot(mixed, (grad_out * gate_row).astype(BF), TN)

    @pl.when(step == 0)
    def _():
        total[...] = jnp.zeros_like(total)
        gate_total[...] = jnp.zeros_like(gate_total)

    total[...] += term
    gate_total[0:1, :] += gate_sum

    @pl.when(step == POS // ROWS - 1)
    def _():
        rows = INNER // DP
        core = place_ref[0]
        table = jnp.concatenate(
            [table_ref[0:2, :], gate_total[0:1, :], jnp.zeros((1, D), F32)], axis=0
        )
        for k in range(CHIPS):
            chip = k % 2 * 4 + k // 2
            both = total[2 * chip * rows : 2 * (chip + 1) * rows, :]
            first = jnp.concatenate([both[:rows], table], axis=0).astype(BF)
            second = jnp.concatenate([both[rows:], table], axis=0).astype(BF)
            keep_ref[k] = jnp.where(core == 0, first, second)
            send_ref[k] = jnp.where(core == 0, second, first)


def output(place, mixed, x, out_grad, modulation, w_out, table):
    half = jax.ShapeDtypeStruct((CHIPS, INNER // DP + 4, D), BF)
    return pl.pallas_call(
        output_kernel,
        grid=(POS // ROWS,),
        in_specs=[
            pl.BlockSpec(memory_space=pltpu.SMEM),
            pl.BlockSpec((ROWS, INNER), lambda j: (j, 0)),
            pl.BlockSpec((ROWS, D), lambda j: (j, 0)),
            pl.BlockSpec((ROWS, D), lambda j: (j, 0)),
            pl.BlockSpec((3, D), lambda j: (0, 0)),
            pl.BlockSpec((INNER, D), lambda j: (0, 0)),
            pl.BlockSpec((8, D), lambda j: (0, 0)),
        ],
        out_specs=[
            pl.BlockSpec((ROWS, D), lambda j: (j, 0)),
            pl.BlockSpec(half.shape, lambda j: (0, 0, 0)),
            pl.BlockSpec(half.shape, lambda j: (0, 0, 0)),
        ],
        out_shape=[jax.ShapeDtypeStruct((POS, D), BF), half, half],
        scratch_shapes=[pltpu.VMEM((INNER, D), F32), pltpu.VMEM((8, D), F32)],
        compiler_params=PARAMS,
        cost_estimate=pl.CostEstimate(
            flops=4 * POS * D * INNER, bytes_accessed=9_000_000, transcendentals=0
        ),
        name="output",
    )(place, mixed, x, out_grad, modulation, w_out, table)


def whole_call(kernel, name, out_shape, *args, scratch=(), smem=0):
    out_specs = jax.tree.map(lambda _: pl.BlockSpec(memory_space=pltpu.VMEM), out_shape)
    return pl.pallas_call(
        kernel,
        in_specs=[pl.BlockSpec(memory_space=pltpu.SMEM)] * smem
        + [pl.BlockSpec(memory_space=pltpu.VMEM)] * (len(args) - smem),
        out_specs=out_specs,
        out_shape=out_shape,
        scratch_shapes=scratch,
        compiler_params=WHOLE,
        cost_estimate=pl.CostEstimate(
            flops=1_000_000, bytes_accessed=sum(2 * a.size for a in args), transcendentals=0
        ),
        name=name,
    )(*args)


def pair_kernel(keep_ref, got_ref, out_ref):
    out_ref[...] = (keep_ref[...].astype(F32) + got_ref[...].astype(F32)).astype(BF)


def pair_sum(keep, got):
    return whole_call(pair_kernel, "pair_sum", jax.ShapeDtypeStruct(keep.shape, BF), keep, got)


def pair_turn_kernel(place_ref, keep_ref, got_ref, *refs):
    total = refs[4]
    total[...] = (keep_ref[...].astype(F32) + got_ref[...].astype(F32)).astype(BF)
    for r in range(4):
        y = lax.rem(place_ref[1] + r, 4)
        for x in range(2):
            refs[r][x] = total[2 * y + x]


def pair_turn(place, keep, got):
    return whole_call(
        pair_turn_kernel,
        "pair_turn",
        [jax.ShapeDtypeStruct((2,) + keep.shape[1:], BF)] * 4,
        place,
        keep,
        got,
        scratch=[pltpu.VMEM(keep.shape, BF)],
        smem=1,
    )


def stacked(block, rows):
    height, width = block.shape
    tiles = [block[:, c : c + 128] for c in range(0, width // 128 * 128, 128)]
    if width % 128:
        last = block[:, width // 128 * 128 :]
        tiles.append(jnp.concatenate([last, jnp.zeros((height, 128 - width % 128), F32)], axis=1))
    tiles.append(jnp.zeros((rows - height * len(tiles), 128), F32))
    return jnp.concatenate(tiles, axis=0)


def unstacked(rows, height, width):
    tiles = [rows[height * c : height * c + height] for c in range(-(-width // 128))]
    return jnp.concatenate(tiles, axis=1)[:, :width]


def pieces_kernel(qkv_ref, o0, o1, o2, o3, pieces_ref):
    parts = []
    for x in range(2):
        out = sum(o[x].astype(F32) for o in (o0, o1, o2, o3))
        parts.append(stacked(qkv_ref[x].astype(F32), SEQ * QKV_ROWS))
        parts.append(stacked(out[: INNER // DP], SEQ * OUT_ROWS))
    table = stacked(jnp.concatenate([out[INNER // DP :], jnp.zeros((4, D), F32)], axis=0)[:3], 32)
    for s in range(SEQ):
        rows = [p[h * s : h * s + h] for p, h in zip(parts, (QKV_ROWS, OUT_ROWS) * 2)]
        pieces_ref[s] = jnp.concatenate(rows + [table], axis=0).astype(BF)


def block_pieces(qkv_blocks, out_blocks):
    return whole_call(
        pieces_kernel,
        "block_pieces",
        jax.ShapeDtypeStruct((SEQ, 2 * BLOCK_ROWS + 32, 128), BF),
        qkv_blocks,
        *out_blocks,
    )


def seq_sum_kernel(factor, place_ref, pieces_ref, own_ref, other_ref):
    total = sum(pieces_ref[k].astype(F32) for k in range(SEQ)) * factor
    first, second = total[:BLOCK_ROWS], total[BLOCK_ROWS : 2 * BLOCK_ROWS]
    table = total[2 * BLOCK_ROWS :]
    own = jnp.where(place_ref[2] == 0, first, second)
    other = jnp.where(place_ref[2] == 0, second, first)
    own_ref[...] = jnp.concatenate([own, table], axis=0)
    other_ref[...] = jnp.concatenate([other, table], axis=0)


def seq_sum(place, pieces, factor):
    return whole_call(
        functools.partial(seq_sum_kernel, factor),
        "seq_sum",
        [jax.ShapeDtypeStruct((BLOCK_ROWS + 32, 128), F32)] * 2,
        place,
        pieces,
        smem=1,
    )


def last_sum_kernel(own_ref, other_ref, pieces_ref, table_ref):
    total = own_ref[...] + other_ref[...]
    piece = total[:BLOCK_ROWS].astype(BF)
    for k in range(DP):
        pieces_ref[k] = piece
    for r in range(3):
        rows = [total[BLOCK_ROWS + 3 * c + r : BLOCK_ROWS + 3 * c + r + 1] for c in range(9)]
        table_ref[r : r + 1, :] = jnp.concatenate(rows, axis=1)


def last_sum(own, other):
    return whole_call(
        last_sum_kernel,
        "last_sum",
        [
            jax.ShapeDtypeStruct((DP, BLOCK_ROWS, 128), BF),
            jax.ShapeDtypeStruct((3, D), F32),
        ],
        own,
        other,
    )


def assemble_kernel(pieces_ref, qkv_ref, out_ref):
    pieces = [pieces_ref[s].astype(F32) for s in range(DP)]
    qkv = jnp.concatenate([p[:QKV_ROWS] for p in pieces], axis=0)
    out = jnp.concatenate([p[QKV_ROWS:] for p in pieces], axis=0)
    qkv_ref[...] = unstacked(qkv, D // SEQ, 3 * INNER)
    out_ref[...] = unstacked(out, INNER // SEQ, D)


def assemble(pieces):
    return whole_call(
        assemble_kernel,
        "assemble",
        [
            jax.ShapeDtypeStruct((D // SEQ, 3 * INNER), F32),
            jax.ShapeDtypeStruct((INNER // SEQ, D), F32),
        ],
        pieces,
    )


def exchange(blocks, axis, groups=None):
    return lax.all_to_all(blocks, axis, 0, 0, axis_index_groups=groups, tiled=True)


def body(clip_tokens, time_mod, mod_table, w_qkv, w_out, out_grad):
    tokens, grad_rows = clip_tokens[0, 0], out_grad[0, 0]
    modulation = mod_table + time_mod[0]
    dp_at = lax.axis_index("dp")
    place = jnp.stack([dp_at % 2, dp_at // 2 % 4, dp_at // 8]).astype(jnp.int32)
    w_turned = w_qkv.T
    x_pos = exchange(tokens.reshape(SEQ, HERE, D), "seq")
    grad_mixed = grad_mixed_rows(grad_rows, modulation, w_out)
    gm_pos = exchange(grad_mixed.reshape(SEQ, HERE, INNER), "seq")
    packed, mixed_pos = forward(x_pos, modulation, w_turned)
    mixed = exchange(mixed_pos, "seq").reshape(POS, INNER)
    delta_pos, qkv_keep, qkv_send, table = backward(
        place, x_pos, gm_pos, packed, modulation, w_turned
    )
    swap = [(i, i ^ 1) for i in range(DP)]
    column = [[8 * x + 2 * y + c for y in range(4)] for x in range(2) for c in range(2)]
    qkv_keep, qkv_send, mixed = lax.optimization_barrier((qkv_keep, qkv_send, mixed))
    qkv_blocks = pair_sum(qkv_keep, lax.ppermute(qkv_send, "dp", swap))
    table = lax.optimization_barrier((table, qkv_blocks))[0]
    qkv_blocks = lax.psum_scatter(
        qkv_blocks, "dp", scatter_dimension=0, axis_index_groups=column, tiled=True
    )
    out_tokens, out_keep, out_send = output(
        place, mixed, tokens, grad_rows, modulation, w_out, table
    )
    out_blocks = list(pair_turn(place, out_keep, lax.ppermute(out_send, "dp", swap)))
    for r in range(1, 4):
        route = [(i, i // 8 * 8 + (i + 2 * r) % 8) for i in range(DP)]
        out_blocks[r] = lax.ppermute(out_blocks[r], "dp", route)
    delta = exchange(delta_pos, "seq")
    pieces, delta = lax.optimization_barrier((block_pieces(qkv_blocks, out_blocks), delta))
    pieces = exchange(pieces, "seq")
    own, other = seq_sum(place, pieces, 1.0 / math.sqrt(DP * SEQ * POS))
    turn = [(i * SEQ + s, s * SEQ + i) for i in range(DP) for s in range(SEQ)]
    turn_other = [(i * SEQ + s, s * SEQ + (i ^ 8)) for i in range(DP) for s in range(SEQ)]
    own = lax.ppermute(own, ("dp", "seq"), turn)
    other = lax.ppermute(other, ("dp", "seq"), turn_other)
    pieces, table = last_sum(own, other)
    qkv_grad, out_weight_grad = assemble(exchange(pieces, "dp"))
    grad_tokens = (grad_rows.astype(F32) + delta.reshape(POS, D).astype(F32)).astype(BF)
    return (
        out_tokens[None, None],
        grad_tokens[None, None],
        qkv_grad,
        out_weight_grad,
        table,
    )


def solution(mesh):
    return jax.shard_map(
        body,
        mesh=mesh,
        in_specs=(
            P("dp", "seq", None, None),
            P("dp", None, None),
            P(),
            P(),
            P(),
            P("dp", "seq", None, None),
        ),
        out_specs=(
            P("dp", "seq", None, None),
            P("dp", "seq", None, None),
            P("seq", None),
            P("seq", None),
            P(),
        ),
        check_vma=False,
    )
```

```python
import functools
import math

import jax
import jax.numpy as jnp
from jax import lax
from jax.experimental import pallas as pl
from jax.experimental.pallas import tpu as pltpu
from jax.sharding import PartitionSpec as P

D = 1152
HEAD_DIM = 72
HEADS = 8
POS = 768
INNER = 576
SEQ = 16
DP = 16
CHIPS = DP // 2
HERE = POS // SEQ
TILE = 16
HALF = 8
ROWS = SEQ * TILE
UNIT = SEQ * HALF
PAIR = 2 * HEAD_DIM
QKV_ROWS = 64
OUT_ROWS = 24
BLOCK_ROWS = QKV_ROWS + OUT_ROWS
STEPS = HERE // TILE
EPSILON = 1e-06
SCALE = 1.0 / math.sqrt(HEAD_DIM)
BF = jnp.bfloat16
F32 = jnp.float32
PARAMS = pltpu.CompilerParams(
    dimension_semantics=("arbitrary",), vmem_limit_bytes=56 * 1024 * 1024
)
WHOLE = pltpu.CompilerParams(vmem_limit_bytes=40 * 1024 * 1024)
NT = (((1,), (1,)), ((), ()))
TN = (((0,), (0,)), ((), ()))


def dot(a, b, dims=(((1,), (0,)), ((), ()))):
    return lax.dot_general(a, b, dims, preferred_element_type=F32)


def normalize(x):
    centered = x - jnp.mean(x, axis=1, keepdims=True)
    inv_std = lax.rsqrt(jnp.mean(centered * centered, axis=1, keepdims=True) + EPSILON)
    return centered * inv_std, inv_std


def load_rows(block):
    wide = block.astype(F32)
    width = wide.shape[-1]
    return jnp.concatenate(
        [wide[:, :HALF].reshape(UNIT, width), wide[:, HALF:].reshape(UNIT, width)], axis=0
    )


def store_rows(rows):
    width = rows.shape[-1]
    halves = [rows[h * UNIT : h * UNIT + UNIT].reshape(SEQ, HALF, width) for h in range(2)]
    return jnp.concatenate(halves, axis=1).astype(BF)


def position_mask():
    rows = lax.broadcasted_iota(jnp.int32, (HALF, UNIT), 0)
    cols = lax.broadcasted_iota(jnp.int32, (HALF, UNIT), 1) % HALF
    return jnp.where(rows == cols, 1.0, 0.0).astype(F32)


def first_lanes(dtype):
    lanes = lax.broadcasted_iota(jnp.int32, (1, PAIR), 1)
    return jnp.where(lanes < HEAD_DIM, 1.0, 0.0).astype(dtype)


def spread(pair, first):
    return jnp.concatenate([pair * first, pair * (1 - first)], axis=0)


def gather(rows, first):
    return rows[:UNIT] * first + rows[UNIT:] * (1 - first)


def by_frame(rows):
    return rows.reshape(2, SEQ, HALF, UNIT)


def softmax(queries, keys_spread, mask):
    scores = by_frame(dot(keys_spread, queries, NT) * SCALE)
    exp_scores = jnp.exp(scores - jnp.max(scores, axis=1, keepdims=True))
    return exp_scores * (mask / jnp.sum(exp_scores, axis=1, keepdims=True))


def flat(weights):
    return weights.reshape(2 * UNIT, UNIT).astype(BF)


def pair_of(rows, part, n):
    start = part * INNER + n * PAIR
    return rows[:, start : start + PAIR]


def forward_kernel(x_ref, mod_ref, w_ref, packed_ref, mixed_ref):
    normed, _ = normalize(load_rows(x_ref[...]))
    modulated = (normed * (1.0 + mod_ref[1:2, :]) + mod_ref[0:1, :]).astype(BF)
    packed = dot(modulated, w_ref[...], NT).astype(BF)
    packed_ref[...] = packed
    mask, first = position_mask(), first_lanes(BF)
    units = []
    for u in range(2):
        rows = packed[u * UNIT : u * UNIT + UNIT]
        pieces = []
        for n in range(HEADS // 2):
            weights = softmax(pair_of(rows, 0, n), spread(pair_of(rows, 1, n), first), mask)
            pieces.append(dot(flat(weights), spread(pair_of(rows, 2, n), first), TN))
        units.append(jnp.concatenate(pieces, axis=1))
    mixed_ref[...] = store_rows(jnp.concatenate(units, axis=0))


def forward(x, modulation, w_turned):
    return pl.pallas_call(
        forward_kernel,
        grid=(STEPS,),
        in_specs=[
            pl.BlockSpec((SEQ, TILE, D), lambda j: (0, j, 0)),
            pl.BlockSpec((3, D), lambda j: (0, 0)),
            pl.BlockSpec((3 * INNER, D), lambda j: (0, 0)),
        ],
        out_specs=[
            pl.BlockSpec((ROWS, 3 * INNER), lambda j: (j, 0)),
            pl.BlockSpec((SEQ, TILE, INNER), lambda j: (0, j, 0)),
        ],
        out_shape=[
            jax.ShapeDtypeStruct((POS, 3 * INNER), BF),
            jax.ShapeDtypeStruct((SEQ, HERE, INNER), BF),
        ],
        compiler_params=PARAMS,
        cost_estimate=pl.CostEstimate(
            flops=2 * POS * D * 3 * INNER * 2, bytes_accessed=12_000_000, transcendentals=800_000
        ),
        name="forward",
    )(x, modulation, w_turned)


def grad_mixed_kernel(grad_ref, mod_ref, w_ref, out_ref):
    grad_branch = (grad_ref[...].astype(F32) * mod_ref[2:3, :]).astype(BF)
    out_ref[...] = dot(grad_branch, w_ref[...], NT).astype(BF)


def grad_mixed_rows(out_grad, modulation, w_out):
    return pl.pallas_call(
        grad_mixed_kernel,
        grid=(POS // ROWS,),
        in_specs=[
            pl.BlockSpec((ROWS, D), lambda j: (j, 0)),
            pl.BlockSpec((3, D), lambda j: (0, 0)),
            pl.BlockSpec((INNER, D), lambda j: (0, 0)),
        ],
        out_specs=pl.BlockSpec((ROWS, INNER), lambda j: (j, 0)),
        out_shape=jax.ShapeDtypeStruct((POS, INNER), BF),
        compiler_params=PARAMS,
        cost_estimate=pl.CostEstimate(
            flops=2 * POS * D * INNER, bytes_accessed=4_000_000, transcendentals=0
        ),
        name="grad_mixed",
    )(out_grad, modulation, w_out)


def backward_kernel(
    x_ref, gm_ref, packed_ref, mod_ref, w_ref,
    delta_ref, blocks_ref, table_ref,
    modulated_all, gp_all, total,
):
    step = pl.program_id(0)
    normed, inv_std = normalize(load_rows(x_ref[...]))
    scale_row = 1.0 + mod_ref[1:2, :]
    here = pl.ds(pl.multiple_of(step * ROWS, ROWS), ROWS)
    modulated_all[here, :] = (normed * scale_row + mod_ref[0:1, :]).astype(BF)
    grad_mixed = load_rows(gm_ref[...]).astype(BF)
    packed = packed_ref[...]
    mask, first, first_wide = position_mask(), first_lanes(BF), first_lanes(F32)
    units = []
    for u in range(2):
        rows = packed[u * UNIT : u * UNIT + UNIT]
        grad_rows = grad_mixed[u * UNIT : u * UNIT + UNIT]
        pieces = [[], [], []]
        for n in range(HEADS // 2):
            queries = pair_of(rows, 0, n)
            keys_spread = spread(pair_of(rows, 1, n), first)
            values_spread = spread(pair_of(rows, 2, n), first)
            grad_pair = pair_of(grad_rows, 0, n)
            weights = softmax(queries, keys_spread, mask)
            grad_weights = by_frame(dot(values_spread, grad_pair, NT))
            row_total = jnp.sum(weights * grad_weights, axis=1, keepdims=True)
            grad_scores = flat(weights * (grad_weights - row_total) * SCALE)
            pieces[0].append(dot(grad_scores, keys_spread, TN).astype(BF))
            pieces[1].append(gather(dot(grad_scores, queries), first_wide).astype(BF))
            pieces[2].append(gather(dot(flat(weights), grad_pair), first_wide).astype(BF))
        units.append(jnp.concatenate(pieces[0] + pieces[1] + pieces[2], axis=1))
    grad_packed = jnp.concatenate(units, axis=0)
    gp_all[here, :] = grad_packed
    grad_mod = dot(grad_packed, w_ref[...])
    shift_sum = jnp.sum(grad_mod, axis=0, keepdims=True)
    scale_sum = jnp.sum(grad_mod * normed, axis=0, keepdims=True)
    grad_normed = grad_mod * scale_row
    delta = inv_std * (
        grad_normed
        - jnp.mean(grad_normed, axis=1, keepdims=True)
        - normed * jnp.mean(grad_normed * normed, axis=1, keepdims=True)
    )
    delta_ref[...] = store_rows(delta)

    @pl.when(step == 0)
    def _():
        table_ref[...] = jnp.zeros_like(table_ref)

    table_ref[0:1, :] += shift_sum
    table_ref[1:2, :] += scale_sum

    @pl.when(step == STEPS - 1)
    def _():
        for r in range(3):
            part = slice(r * 384, r * 384 + 384)
            total[part, :] = dot(modulated_all[:, part], gp_all[...], TN)
        rows = D // DP
        for i in range(DP):
            blocks_ref[i % 8 * 2 + i // 8] = total[rows * i : rows * i + rows, :].astype(BF)


def backward(x, grad_mixed, packed, modulation, w_turned):
    blocks = jax.ShapeDtypeStruct((DP, D // DP, 3 * INNER), BF)
    return pl.pallas_call(
        backward_kernel,
        grid=(STEPS,),
        in_specs=[
            pl.BlockSpec((SEQ, TILE, D), lambda j: (0, j, 0)),
            pl.BlockSpec((SEQ, TILE, INNER), lambda j: (0, j, 0)),
            pl.BlockSpec((ROWS, 3 * INNER), lambda j: (j, 0)),
            pl.BlockSpec((3, D), lambda j: (0, 0)),
            pl.BlockSpec((3 * INNER, D), lambda j: (0, 0)),
        ],
        out_specs=[
            pl.BlockSpec((SEQ, TILE, D), lambda j: (0, j, 0)),
            pl.BlockSpec(blocks.shape, lambda j: (0, 0, 0)),
            pl.BlockSpec((8, D), lambda j: (0, 0)),
        ],
        out_shape=[
            jax.ShapeDtypeStruct((SEQ, HERE, D), BF),
            blocks,
            jax.ShapeDtypeStruct((8, D), F32),
        ],
        scratch_shapes=[
            pltpu.VMEM((POS, D), BF),
            pltpu.VMEM((POS, 3 * INNER), BF),
            pltpu.VMEM((D, 3 * INNER), F32),
        ],
        compiler_params=PARAMS,
        cost_estimate=pl.CostEstimate(
            flops=2 * POS * D * 3 * INNER * 4, bytes_accessed=20_000_000, transcendentals=800_000
        ),
        name="backward",
    )(x, grad_mixed, packed, modulation, w_turned)


def output_kernel(
    place_ref, mixed_ref, x_ref, grad_ref, mod_ref, w_ref, table_ref,
    out_ref, keep_ref, send_ref, total, gate_total,
):
    step = pl.program_id(0)
    gate_row = mod_ref[2:3, :]
    mixed = mixed_ref[...]
    branch = dot(mixed, w_ref[...])
    out_ref[...] = (x_ref[...].astype(F32) + gate_row * branch).astype(BF)
    grad_out = grad_ref[...].astype(F32)
    gate_sum = jnp.sum(grad_out * branch, axis=0, keepdims=True)
    term = dot(mixed, (grad_out * gate_row).astype(BF), TN)

    @pl.when(step == 0)
    def _():
        total[...] = jnp.zeros_like(total)
        gate_total[...] = jnp.zeros_like(gate_total)

    total[...] += term
    gate_total[0:1, :] += gate_sum

    @pl.when(step == POS // ROWS - 1)
    def _():
        rows = INNER // DP
        core = place_ref[0]
        table = jnp.concatenate(
            [table_ref[0:2, :], gate_total[0:1, :], jnp.zeros((1, D), F32)], axis=0
        )
        for k in range(CHIPS):
            chip = k % 2 * 4 + k // 2
            both = total[2 * chip * rows : 2 * (chip + 1) * rows, :]
            first = jnp.concatenate([both[:rows], table], axis=0).astype(BF)
            second = jnp.concatenate([both[rows:], table], axis=0).astype(BF)
            keep_ref[k] = jnp.where(core == 0, first, second)
            send_ref[k] = jnp.where(core == 0, second, first)


def output(place, mixed, x, out_grad, modulation, w_out, table):
    half = jax.ShapeDtypeStruct((CHIPS, INNER // DP + 4, D), BF)
    return pl.pallas_call(
        output_kernel,
        grid=(POS // ROWS,),
        in_specs=[
            pl.BlockSpec(memory_space=pltpu.SMEM),
            pl.BlockSpec((ROWS, INNER), lambda j: (j, 0)),
            pl.BlockSpec((ROWS, D), lambda j: (j, 0)),
            pl.BlockSpec((ROWS, D), lambda j: (j, 0)),
            pl.BlockSpec((3, D), lambda j: (0, 0)),
            pl.BlockSpec((INNER, D), lambda j: (0, 0)),
            pl.BlockSpec((8, D), lambda j: (0, 0)),
        ],
        out_specs=[
            pl.BlockSpec((ROWS, D), lambda j: (j, 0)),
            pl.BlockSpec(half.shape, lambda j: (0, 0, 0)),
            pl.BlockSpec(half.shape, lambda j: (0, 0, 0)),
        ],
        out_shape=[jax.ShapeDtypeStruct((POS, D), BF), half, half],
        scratch_shapes=[pltpu.VMEM((INNER, D), F32), pltpu.VMEM((8, D), F32)],
        compiler_params=PARAMS,
        cost_estimate=pl.CostEstimate(
            flops=4 * POS * D * INNER, bytes_accessed=9_000_000, transcendentals=0
        ),
        name="output",
    )(place, mixed, x, out_grad, modulation, w_out, table)


def whole_call(kernel, name, out_shape, *args, scratch=(), smem=0):
    out_specs = jax.tree.map(lambda _: pl.BlockSpec(memory_space=pltpu.VMEM), out_shape)
    return pl.pallas_call(
        kernel,
        in_specs=[pl.BlockSpec(memory_space=pltpu.SMEM)] * smem
        + [pl.BlockSpec(memory_space=pltpu.VMEM)] * (len(args) - smem),
        out_specs=out_specs,
        out_shape=out_shape,
        scratch_shapes=scratch,
        compiler_params=WHOLE,
        cost_estimate=pl.CostEstimate(
            flops=1_000_000, bytes_accessed=sum(2 * a.size for a in args), transcendentals=0
        ),
        name=name,
    )(*args)


def pair_turn_kernel(place_ref, keep_ref, got_ref, *refs):
    total = refs[4]
    total[...] = (keep_ref[...].astype(F32) + got_ref[...].astype(F32)).astype(BF)
    for r in range(4):
        y = lax.rem(place_ref[1] + r, 4)
        for x in range(2):
            refs[r][x] = total[2 * y + x]


def pair_turn(place, keep, got):
    return whole_call(
        pair_turn_kernel,
        "pair_turn",
        [jax.ShapeDtypeStruct((2,) + keep.shape[1:], BF)] * 4,
        place,
        keep,
        got,
        scratch=[pltpu.VMEM(keep.shape, BF)],
        smem=1,
    )


def stacked(block, rows):
    height, width = block.shape
    tiles = [block[:, c : c + 128] for c in range(0, width // 128 * 128, 128)]
    if width % 128:
        last = block[:, width // 128 * 128 :]
        tiles.append(jnp.concatenate([last, jnp.zeros((height, 128 - width % 128), F32)], axis=1))
    tiles.append(jnp.zeros((rows - height * len(tiles), 128), F32))
    return jnp.concatenate(tiles, axis=0)


def unstacked(rows, height, width):
    tiles = [rows[height * c : height * c + height] for c in range(-(-width // 128))]
    return jnp.concatenate(tiles, axis=1)[:, :width]


def pieces_kernel(qkv_ref, o0, o1, o2, o3, pieces_ref):
    parts = []
    for x in range(2):
        out = (o0[x].astype(F32) + o2[x].astype(F32)) + (o1[x].astype(F32) + o3[x].astype(F32))
        parts.append(stacked(qkv_ref[x].astype(F32), SEQ * QKV_ROWS))
        parts.append(stacked(out[: INNER // DP], SEQ * OUT_ROWS))
    table = stacked(jnp.concatenate([out[INNER // DP :], jnp.zeros((4, D), F32)], axis=0)[:3], 32)
    for s in range(SEQ):
        rows = [p[h * s : h * s + h] for p, h in zip(parts, (QKV_ROWS, OUT_ROWS) * 2)]
        rows += [table[2 * s : 2 * s + 2], jnp.zeros((6, 128), F32)]
        pieces_ref[s] = jnp.concatenate(rows, axis=0).astype(BF)


def block_pieces(qkv_blocks, out_blocks):
    return whole_call(
        pieces_kernel,
        "block_pieces",
        jax.ShapeDtypeStruct((SEQ, 2 * BLOCK_ROWS + 8, 128), BF),
        qkv_blocks,
        *out_blocks,
    )


def seq_sum_kernel(factor, place_ref, pieces_ref, own_ref, other_ref):
    total = sum(pieces_ref[k].astype(F32) for k in range(SEQ)) * factor
    first, second = total[:BLOCK_ROWS], total[BLOCK_ROWS : 2 * BLOCK_ROWS]
    table = total[2 * BLOCK_ROWS :]
    own = jnp.where(place_ref[2] == 0, first, second)
    other = jnp.where(place_ref[2] == 0, second, first)
    own_ref[...] = jnp.concatenate([own, table], axis=0)
    other_ref[...] = jnp.concatenate([other, table], axis=0)


def seq_sum(place, pieces, factor):
    return whole_call(
        functools.partial(seq_sum_kernel, factor),
        "seq_sum",
        [jax.ShapeDtypeStruct((BLOCK_ROWS + 8, 128), F32)] * 2,
        place,
        pieces,
        smem=1,
    )


def last_sum_kernel(own_ref, other_ref, pieces_ref):
    piece = (own_ref[...] + other_ref[...]).astype(BF)
    for k in range(DP):
        pieces_ref[k] = piece


def last_sum(own, other):
    return whole_call(
        last_sum_kernel,
        "last_sum",
        jax.ShapeDtypeStruct((DP, BLOCK_ROWS + 8, 128), BF),
        own,
        other,
    )


def assemble_kernel(pieces_ref, qkv_ref, out_ref, table_ref):
    pieces = [pieces_ref[s].astype(F32) for s in range(DP)]
    qkv = jnp.concatenate([p[:QKV_ROWS] for p in pieces], axis=0)
    out = jnp.concatenate([p[QKV_ROWS:BLOCK_ROWS] for p in pieces], axis=0)
    table = jnp.concatenate([p[BLOCK_ROWS : BLOCK_ROWS + 2] for p in pieces], axis=0)
    qkv_ref[...] = unstacked(qkv, D // SEQ, 3 * INNER)
    out_ref[...] = unstacked(out, INNER // SEQ, D)
    table_ref[...] = unstacked(table, 3, D)


def assemble(pieces):
    return whole_call(
        assemble_kernel,
        "assemble",
        [
            jax.ShapeDtypeStruct((D // SEQ, 3 * INNER), F32),
            jax.ShapeDtypeStruct((INNER // SEQ, D), F32),
            jax.ShapeDtypeStruct((3, D), F32),
        ],
        pieces,
    )


def exchange(blocks, axis, groups=None):
    return lax.all_to_all(blocks, axis, 0, 0, axis_index_groups=groups, tiled=True)


def body(clip_tokens, time_mod, mod_table, w_qkv, w_out, out_grad):
    tokens, grad_rows = clip_tokens[0, 0], out_grad[0, 0]
    modulation = mod_table + time_mod[0]
    dp_at = lax.axis_index("dp")
    place = jnp.stack([dp_at % 2, dp_at // 2 % 4, dp_at // 8]).astype(jnp.int32)
    w_turned = w_qkv.T
    x_pos = exchange(tokens.reshape(SEQ, HERE, D), "seq")
    grad_mixed = grad_mixed_rows(grad_rows, modulation, w_out)
    gm_pos = exchange(grad_mixed.reshape(SEQ, HERE, INNER), "seq")
    packed, mixed_pos = forward(x_pos, modulation, w_turned)
    mixed = exchange(mixed_pos, "seq").reshape(POS, INNER)
    delta_pos, qkv_blocks, table = backward(x_pos, gm_pos, packed, modulation, w_turned)
    column = [[8 * x + i for i in range(8)] for x in range(2)]
    qkv_blocks, mixed = lax.optimization_barrier((qkv_blocks, mixed))
    qkv_blocks = lax.psum_scatter(
        qkv_blocks, "dp", scatter_dimension=0, axis_index_groups=column, tiled=True
    )
    out_tokens, out_keep, out_send = output(
        place, mixed, tokens, grad_rows, modulation, w_out, table
    )
    swap = [(i, i ^ 1) for i in range(DP)]
    out_blocks = list(pair_turn(place, out_keep, lax.ppermute(out_send, "dp", swap)))
    for r in range(1, 4):
        route = [(i, i // 8 * 8 + (i + 2 * r) % 8) for i in range(DP)]
        out_blocks[r] = lax.ppermute(out_blocks[r], "dp", route)
    delta = exchange(delta_pos, "seq")
    pieces, delta = lax.optimization_barrier((block_pieces(qkv_blocks, out_blocks), delta))
    pieces = exchange(pieces, "seq")
    own, other = seq_sum(place, pieces, 1.0 / math.sqrt(DP * SEQ * POS))
    turn = [(i * SEQ + s, s * SEQ + i) for i in range(DP) for s in range(SEQ)]
    turn_other = [(i * SEQ + s, s * SEQ + (i ^ 8)) for i in range(DP) for s in range(SEQ)]
    own = lax.ppermute(own, ("dp", "seq"), turn)
    other = lax.ppermute(other, ("dp", "seq"), turn_other)
    pieces = exchange(last_sum(own, other), "dp")
    qkv_grad, out_weight_grad, table = assemble(pieces)
    grad_tokens = (grad_rows.astype(F32) + delta.reshape(POS, D).astype(F32)).astype(BF)
    return (
        out_tokens[None, None],
        grad_tokens[None, None],
        qkv_grad,
        out_weight_grad,
        table,
    )


def solution(mesh):
    return jax.shard_map(
        body,
        mesh=mesh,
        in_specs=(
            P("dp", "seq", None, None),
            P("dp", None, None),
            P(),
            P(),
            P(),
            P("dp", "seq", None, None),
        ),
        out_specs=(
            P("dp", "seq", None, None),
            P("dp", "seq", None, None),
            P("seq", None),
            P("seq", None),
            P(),
        ),
        check_vma=False,
    )
```

```python
import functools
import math

import jax
import jax.numpy as jnp
from jax import lax
from jax.experimental import pallas as pl
from jax.experimental.pallas import tpu as pltpu
from jax.sharding import PartitionSpec as P

D = 1152
HEAD_DIM = 72
HEADS = 8
POS = 768
INNER = 576
SEQ = 16
DP = 16
HERE = POS // SEQ
TILE = 16
HALF = 8
ROWS = SEQ * TILE
UNIT = SEQ * HALF
PAIR = 2 * HEAD_DIM
CHUNKS = 8
LANES = 256
QKV_LANES = 3 * INNER // CHUNKS
OUT_LANES = D // CHUNKS
OUT_HEIGHT = INNER + 16
PIECE_ROWS = 184
STEPS = HERE // TILE
EPSILON = 1e-06
SCALE = 1.0 / math.sqrt(HEAD_DIM)
BF = jnp.bfloat16
F32 = jnp.float32
PARAMS = pltpu.CompilerParams(
    dimension_semantics=("arbitrary",), vmem_limit_bytes=56 * 1024 * 1024
)
WHOLE = pltpu.CompilerParams(vmem_limit_bytes=40 * 1024 * 1024)
NT = (((1,), (1,)), ((), ()))
TN = (((0,), (0,)), ((), ()))


def dot(a, b, dims=(((1,), (0,)), ((), ()))):
    return lax.dot_general(a, b, dims, preferred_element_type=F32)


def normalize(x):
    centered = x - jnp.mean(x, axis=1, keepdims=True)
    inv_std = lax.rsqrt(jnp.mean(centered * centered, axis=1, keepdims=True) + EPSILON)
    return centered * inv_std, inv_std


def load_rows(block):
    wide = block.astype(F32)
    width = wide.shape[-1]
    return jnp.concatenate(
        [wide[:, :HALF].reshape(UNIT, width), wide[:, HALF:].reshape(UNIT, width)], axis=0
    )


def store_rows(rows):
    width = rows.shape[-1]
    halves = [rows[h * UNIT : h * UNIT + UNIT].reshape(SEQ, HALF, width) for h in range(2)]
    return jnp.concatenate(halves, axis=1).astype(BF)


def position_mask():
    rows = lax.broadcasted_iota(jnp.int32, (HALF, UNIT), 0)
    cols = lax.broadcasted_iota(jnp.int32, (HALF, UNIT), 1) % HALF
    return jnp.where(rows == cols, 1.0, 0.0).astype(F32)


def first_lanes(dtype):
    lanes = lax.broadcasted_iota(jnp.int32, (1, PAIR), 1)
    return jnp.where(lanes < HEAD_DIM, 1.0, 0.0).astype(dtype)


def spread(pair, first):
    return jnp.concatenate([pair * first, pair * (1 - first)], axis=0)


def gather(rows, first):
    return rows[:UNIT] * first + rows[UNIT:] * (1 - first)


def by_frame(rows):
    return rows.reshape(2, SEQ, HALF, UNIT)


def softmax(queries, keys_spread, mask):
    scores = by_frame(dot(keys_spread, queries, NT) * SCALE)
    exp_scores = jnp.exp(scores - jnp.max(scores, axis=1, keepdims=True))
    return exp_scores * (mask / jnp.sum(exp_scores, axis=1, keepdims=True))


def flat(weights):
    return weights.reshape(2 * UNIT, UNIT).astype(BF)


def pair_of(rows, part, n):
    start = part * INNER + n * PAIR
    return rows[:, start : start + PAIR]


def forward_kernel(x_ref, mod_ref, w_ref, packed_ref, mixed_ref):
    normed, _ = normalize(load_rows(x_ref[...]))
    modulated = (normed * (1.0 + mod_ref[1:2, :]) + mod_ref[0:1, :]).astype(BF)
    packed = dot(modulated, w_ref[...], NT).astype(BF)
    packed_ref[...] = packed
    mask, first = position_mask(), first_lanes(BF)
    units = []
    for u in range(2):
        rows = packed[u * UNIT : u * UNIT + UNIT]
        pieces = []
        for n in range(HEADS // 2):
            weights = softmax(pair_of(rows, 0, n), spread(pair_of(rows, 1, n), first), mask)
            pieces.append(dot(flat(weights), spread(pair_of(rows, 2, n), first), TN))
        units.append(jnp.concatenate(pieces, axis=1))
    mixed_ref[...] = store_rows(jnp.concatenate(units, axis=0))


def forward(x, modulation, w_turned):
    return pl.pallas_call(
        forward_kernel,
        grid=(STEPS,),
        in_specs=[
            pl.BlockSpec((SEQ, TILE, D), lambda j: (0, j, 0)),
            pl.BlockSpec((3, D), lambda j: (0, 0)),
            pl.BlockSpec((3 * INNER, D), lambda j: (0, 0)),
        ],
        out_specs=[
            pl.BlockSpec((ROWS, 3 * INNER), lambda j: (j, 0)),
            pl.BlockSpec((SEQ, TILE, INNER), lambda j: (0, j, 0)),
        ],
        out_shape=[
            jax.ShapeDtypeStruct((POS, 3 * INNER), BF),
            jax.ShapeDtypeStruct((SEQ, HERE, INNER), BF),
        ],
        compiler_params=PARAMS,
        cost_estimate=pl.CostEstimate(
            flops=2 * POS * D * 3 * INNER * 2, bytes_accessed=12_000_000, transcendentals=800_000
        ),
        name="forward",
    )(x, modulation, w_turned)


def grad_mixed_kernel(grad_ref, mod_ref, w_ref, out_ref):
    grad_branch = (grad_ref[...].astype(F32) * mod_ref[2:3, :]).astype(BF)
    out_ref[...] = dot(grad_branch, w_ref[...], NT).astype(BF)


def grad_mixed_rows(out_grad, modulation, w_out):
    return pl.pallas_call(
        grad_mixed_kernel,
        grid=(POS // ROWS,),
        in_specs=[
            pl.BlockSpec((ROWS, D), lambda j: (j, 0)),
            pl.BlockSpec((3, D), lambda j: (0, 0)),
            pl.BlockSpec((INNER, D), lambda j: (0, 0)),
        ],
        out_specs=pl.BlockSpec((ROWS, INNER), lambda j: (j, 0)),
        out_shape=jax.ShapeDtypeStruct((POS, INNER), BF),
        compiler_params=PARAMS,
        cost_estimate=pl.CostEstimate(
            flops=2 * POS * D * INNER, bytes_accessed=4_000_000, transcendentals=0
        ),
        name="grad_mixed",
    )(out_grad, modulation, w_out)


def chunk_of(rows, m, lanes):
    pad = jnp.zeros((rows.shape[0], LANES - lanes), rows.dtype)
    return jnp.concatenate([rows[:, lanes * m : lanes * m + lanes], pad], axis=1)


def backward_kernel(
    x_ref, gm_ref, packed_ref, mod_ref, w_ref,
    delta_ref, blocks_ref, table_ref,
    modulated_all, gp_all,
):
    step = pl.program_id(0)
    normed, inv_std = normalize(load_rows(x_ref[...]))
    scale_row = 1.0 + mod_ref[1:2, :]
    here = pl.ds(pl.multiple_of(step * ROWS, ROWS), ROWS)
    modulated_all[here, :] = (normed * scale_row + mod_ref[0:1, :]).astype(BF)
    grad_mixed = load_rows(gm_ref[...]).astype(BF)
    packed = packed_ref[...]
    mask, first, first_wide = position_mask(), first_lanes(BF), first_lanes(F32)
    units = []
    for u in range(2):
        rows = packed[u * UNIT : u * UNIT + UNIT]
        grad_rows = grad_mixed[u * UNIT : u * UNIT + UNIT]
        pieces = [[], [], []]
        for n in range(HEADS // 2):
            queries = pair_of(rows, 0, n)
            keys_spread = spread(pair_of(rows, 1, n), first)
            values_spread = spread(pair_of(rows, 2, n), first)
            grad_pair = pair_of(grad_rows, 0, n)
            weights = softmax(queries, keys_spread, mask)
            grad_weights = by_frame(dot(values_spread, grad_pair, NT))
            row_total = jnp.sum(weights * grad_weights, axis=1, keepdims=True)
            grad_scores = flat(weights * (grad_weights - row_total) * SCALE)
            pieces[0].append(dot(grad_scores, keys_spread, TN).astype(BF))
            pieces[1].append(gather(dot(grad_scores, queries), first_wide).astype(BF))
            pieces[2].append(gather(dot(flat(weights), grad_pair), first_wide).astype(BF))
        units.append(jnp.concatenate(pieces[0] + pieces[1] + pieces[2], axis=1))
    grad_packed = jnp.concatenate(units, axis=0)
    for m in range(CHUNKS):
        gp_all[here, LANES * m : LANES * m + LANES] = chunk_of(grad_packed, m, QKV_LANES)
    grad_mod = dot(grad_packed, w_ref[...])
    shift_sum = jnp.sum(grad_mod, axis=0, keepdims=True)
    scale_sum = jnp.sum(grad_mod * normed, axis=0, keepdims=True)
    grad_normed = grad_mod * scale_row
    delta = inv_std * (
        grad_normed
        - jnp.mean(grad_normed, axis=1, keepdims=True)
        - normed * jnp.mean(grad_normed * normed, axis=1, keepdims=True)
    )
    delta_ref[...] = store_rows(delta)

    @pl.when(step == 0)
    def _():
        table_ref[...] = jnp.zeros_like(table_ref)

    table_ref[0:1, :] += shift_sum
    table_ref[1:2, :] += scale_sum

    @pl.when(step == STEPS - 1)
    def _():
        for r in range(3):
            part = slice(r * 384, r * 384 + 384)
            total = dot(modulated_all[:, part], gp_all[...], TN)
            for m in range(CHUNKS):
                blocks_ref[m, part, :] = total[:, LANES * m : LANES * m + LANES].astype(BF)


def backward(x, grad_mixed, packed, modulation, w_turned):
    blocks = jax.ShapeDtypeStruct((CHUNKS, D, LANES), BF)
    return pl.pallas_call(
        backward_kernel,
        grid=(STEPS,),
        in_specs=[
            pl.BlockSpec((SEQ, TILE, D), lambda j: (0, j, 0)),
            pl.BlockSpec((SEQ, TILE, INNER), lambda j: (0, j, 0)),
            pl.BlockSpec((ROWS, 3 * INNER), lambda j: (j, 0)),
            pl.BlockSpec((3, D), lambda j: (0, 0)),
            pl.BlockSpec((3 * INNER, D), lambda j: (0, 0)),
        ],
        out_specs=[
            pl.BlockSpec((SEQ, TILE, D), lambda j: (0, j, 0)),
            pl.BlockSpec(blocks.shape, lambda j: (0, 0, 0)),
            pl.BlockSpec((8, D), lambda j: (0, 0)),
        ],
        out_shape=[
            jax.ShapeDtypeStruct((SEQ, HERE, D), BF),
            blocks,
            jax.ShapeDtypeStruct((8, D), F32),
        ],
        scratch_shapes=[
            pltpu.VMEM((POS, D), BF),
            pltpu.VMEM((POS, CHUNKS * LANES), BF),
        ],
        compiler_params=PARAMS,
        cost_estimate=pl.CostEstimate(
            flops=2 * POS * D * 3 * INNER * 4, bytes_accessed=20_000_000, transcendentals=800_000
        ),
        name="backward",
    )(x, grad_mixed, packed, modulation, w_turned)


def output_kernel(
    place_ref, mixed_ref, x_ref, grad_ref, mod_ref, w_ref, table_ref,
    out_ref, keep_ref, send_ref, total, gate_total,
):
    step = pl.program_id(0)
    gate_row = mod_ref[2:3, :]
    mixed = mixed_ref[...]
    branch = dot(mixed, w_ref[...])
    out_ref[...] = (x_ref[...].astype(F32) + gate_row * branch).astype(BF)
    grad_out = grad_ref[...].astype(F32)
    gate_sum = jnp.sum(grad_out * branch, axis=0, keepdims=True)
    grad_branch = (grad_out * gate_row).astype(BF)
    chunks = [chunk_of(grad_branch, m, OUT_LANES) for m in range(CHUNKS)]
    term = dot(mixed, jnp.concatenate(chunks, axis=1), TN)

    @pl.when(step == 0)
    def _():
        total[...] = jnp.zeros_like(total)
        gate_total[...] = jnp.zeros_like(gate_total)

    total[...] += term
    gate_total[0:1, :] += gate_sum

    @pl.when(step == POS // ROWS - 1)
    def _():
        table = jnp.concatenate(
            [table_ref[0:2, :], gate_total[0:1, :], jnp.zeros((13, D), F32)], axis=0
        )
        first_core = place_ref[0] == 0
        for y in range(CHUNKS // 2):
            for part, pair in (
                (slice(0, INNER), [total[:, LANES * m : LANES * m + LANES] for m in (2 * y, 2 * y + 1)]),
                (slice(INNER, OUT_HEIGHT), [chunk_of(table, m, OUT_LANES) for m in (2 * y, 2 * y + 1)]),
            ):
                keep_ref[y, part, :] = jnp.where(first_core, pair[0], pair[1]).astype(BF)
                send_ref[y, part, :] = jnp.where(first_core, pair[1], pair[0]).astype(BF)


def output(place, mixed, x, out_grad, modulation, w_out, table):
    half = jax.ShapeDtypeStruct((CHUNKS // 2, OUT_HEIGHT, LANES), BF)
    return pl.pallas_call(
        output_kernel,
        grid=(POS // ROWS,),
        in_specs=[
            pl.BlockSpec(memory_space=pltpu.SMEM),
            pl.BlockSpec((ROWS, INNER), lambda j: (j, 0)),
            pl.BlockSpec((ROWS, D), lambda j: (j, 0)),
            pl.BlockSpec((ROWS, D), lambda j: (j, 0)),
            pl.BlockSpec((3, D), lambda j: (0, 0)),
            pl.BlockSpec((INNER, D), lambda j: (0, 0)),
            pl.BlockSpec((8, D), lambda j: (0, 0)),
        ],
        out_specs=[
            pl.BlockSpec((ROWS, D), lambda j: (j, 0)),
            pl.BlockSpec(half.shape, lambda j: (0, 0, 0)),
            pl.BlockSpec(half.shape, lambda j: (0, 0, 0)),
        ],
        out_shape=[jax.ShapeDtypeStruct((POS, D), BF), half, half],
        scratch_shapes=[pltpu.VMEM((INNER, CHUNKS * LANES), F32), pltpu.VMEM((8, D), F32)],
        compiler_params=PARAMS,
        cost_estimate=pl.CostEstimate(
            flops=4 * POS * D * INNER, bytes_accessed=9_000_000, transcendentals=0
        ),
        name="output",
    )(place, mixed, x, out_grad, modulation, w_out, table)


def whole_call(kernel, name, out_shape, *args, scratch=(), smem=0):
    out_specs = jax.tree.map(lambda _: pl.BlockSpec(memory_space=pltpu.VMEM), out_shape)
    return pl.pallas_call(
        kernel,
        in_specs=[pl.BlockSpec(memory_space=pltpu.SMEM)] * smem
        + [pl.BlockSpec(memory_space=pltpu.VMEM)] * (len(args) - smem),
        out_specs=out_specs,
        out_shape=out_shape,
        scratch_shapes=scratch,
        compiler_params=WHOLE,
        cost_estimate=pl.CostEstimate(
            flops=1_000_000, bytes_accessed=sum(2 * a.size for a in args), transcendentals=0
        ),
        name=name,
    )(*args)


def pair_turn_kernel(place_ref, keep_ref, got_ref, *refs):
    total = refs[4]
    total[...] = (keep_ref[...].astype(F32) + got_ref[...].astype(F32)).astype(BF)
    for r in range(4):
        refs[r][...] = total[lax.rem(place_ref[1] + r, 4)]


def pair_turn(place, keep, got):
    return whole_call(
        pair_turn_kernel,
        "pair_turn",
        [jax.ShapeDtypeStruct(keep.shape[1:], BF)] * 4,
        place,
        keep,
        got,
        scratch=[pltpu.VMEM(keep.shape, BF)],
        smem=1,
    )


def pieces_kernel(qkv_ref, o0, o1, o2, o3, pieces_ref):
    qkv = qkv_ref[0].astype(F32)
    out = (o0[...].astype(F32) + o2[...].astype(F32)) + (o1[...].astype(F32) + o3[...].astype(F32))
    table = out[INNER : INNER + 3]
    rows, out_rows = D // SEQ, INNER // SEQ
    for t in range(SEQ):
        q = qkv[rows * t : rows * t + rows]
        w = out[out_rows * t : out_rows * t + out_rows]
        side = [w[:, 128:OUT_LANES], table[:, 128:OUT_LANES], jnp.zeros((33, 16), F32)]
        right = [q[:, 128:QKV_LANES], jnp.concatenate(side, axis=0), jnp.zeros((rows, 24), F32)]
        piece = [q[:, :128], jnp.concatenate(right, axis=1)]
        piece += [w[:, :128], table[:, :128], jnp.zeros((1, 128), F32)]
        pieces_ref[t] = jnp.concatenate(piece, axis=0).astype(BF)


def block_pieces(qkv_chunk, out_chunks):
    return whole_call(
        pieces_kernel,
        "block_pieces",
        jax.ShapeDtypeStruct((SEQ, PIECE_ROWS, 128), BF),
        qkv_chunk,
        *out_chunks,
    )


def seq_sum_kernel(factor, got_ref, pieces_ref):
    piece = (sum(got_ref[k].astype(F32) for k in range(SEQ)) * factor).astype(BF)
    for k in range(DP):
        pieces_ref[k] = piece


def seq_sum(got, factor):
    return whole_call(
        functools.partial(seq_sum_kernel, factor),
        "seq_sum",
        jax.ShapeDtypeStruct((DP, PIECE_ROWS, 128), BF),
        got,
    )


def assemble_kernel(pieces_ref, qkv_ref, out_ref, table_ref):
    qkv, out, table = [], [], []
    for m in range(CHUNKS):
        p = pieces_ref[m].astype(F32) + pieces_ref[CHUNKS + m].astype(F32)
        qkv += [p[0:72], p[72:144, 0:88]]
        out += [p[144:180], p[72:108, 88:104]]
        table += [p[180:183], p[108:111, 88:104]]
    qkv_ref[...] = jnp.concatenate(qkv, axis=1)
    out_ref[...] = jnp.concatenate(out, axis=1)
    table_ref[...] = jnp.concatenate(table, axis=1)


def assemble(pieces):
    return whole_call(
        assemble_kernel,
        "assemble",
        [
            jax.ShapeDtypeStruct((D // SEQ, 3 * INNER), F32),
            jax.ShapeDtypeStruct((INNER // SEQ, D), F32),
            jax.ShapeDtypeStruct((3, D), F32),
        ],
        pieces,
    )


def exchange(blocks, axis, groups=None):
    return lax.all_to_all(blocks, axis, 0, 0, axis_index_groups=groups, tiled=True)


def body(clip_tokens, time_mod, mod_table, w_qkv, w_out, out_grad):
    tokens, grad_rows = clip_tokens[0, 0], out_grad[0, 0]
    modulation = mod_table + time_mod[0]
    dp_at = lax.axis_index("dp")
    place = jnp.stack([dp_at % 2, dp_at // 2 % 4]).astype(jnp.int32)
    w_turned = w_qkv.T
    x_pos = exchange(tokens.reshape(SEQ, HERE, D), "seq")
    grad_mixed = grad_mixed_rows(grad_rows, modulation, w_out)
    gm_pos = exchange(grad_mixed.reshape(SEQ, HERE, INNER), "seq")
    packed, mixed_pos = forward(x_pos, modulation, w_turned)
    mixed = exchange(mixed_pos, "seq").reshape(POS, INNER)
    delta_pos, qkv_blocks, table = backward(x_pos, gm_pos, packed, modulation, w_turned)
    column = [[8 * x + i for i in range(8)] for x in range(2)]
    qkv_blocks, mixed = lax.optimization_barrier((qkv_blocks, mixed))
    qkv_blocks = lax.psum_scatter(
        qkv_blocks, "dp", scatter_dimension=0, axis_index_groups=column, tiled=True
    )
    out_tokens, out_keep, out_send = output(
        place, mixed, tokens, grad_rows, modulation, w_out, table
    )
    swap = [(i, i ^ 1) for i in range(DP)]
    out_blocks = list(pair_turn(place, out_keep, lax.ppermute(out_send, "dp", swap)))
    for r in range(1, 4):
        route = [(i, i // 8 * 8 + (i + 2 * r) % 8) for i in range(DP)]
        out_blocks[r] = lax.ppermute(out_blocks[r], "dp", route)
    delta = exchange(delta_pos, "seq")
    pieces, delta = lax.optimization_barrier((block_pieces(qkv_blocks, out_blocks), delta))
    pieces = exchange(pieces, "seq")
    pieces = exchange(seq_sum(pieces, 1.0 / math.sqrt(DP * SEQ * POS)), "dp")
    qkv_grad, out_weight_grad, table = assemble(pieces)
    grad_tokens = (grad_rows.astype(F32) + delta.reshape(POS, D).astype(F32)).astype(BF)
    return (
        out_tokens[None, None],
        grad_tokens[None, None],
        qkv_grad,
        out_weight_grad,
        table,
    )


def solution(mesh):
    return jax.shard_map(
        body,
        mesh=mesh,
        in_specs=(
            P("dp", "seq", None, None),
            P("dp", None, None),
            P(),
            P(),
            P(),
            P("dp", "seq", None, None),
        ),
        out_specs=(
            P("dp", "seq", None, None),
            P("dp", "seq", None, None),
            P("seq", None),
            P("seq", None),
            P(),
        ),
        check_vma=False,
    )
```
